256 devices in a mesh: seq: 16 (over z, x_lo), res: 16 (over x_hi, y, core).
Axes of the slice: x: 4 (x_hi: 2, x_lo: 2; x = x_hi * 2 + x_lo), y: 4, z: 8, core: 2. Of those that a mesh axis runs over, the one named last changes fastest.
Arguments:
- homolog_embedding: bfloat16 [160, 2048, 256], P('seq', 'res'), may hold values from -6 to 6
- contact_embedding: bfloat16 [2048, 2048, 128], P('seq', 'res'), may hold values from -6 to 6
- homolog_scaling_factor: float32 [256], replicated, may hold values from 0.5 to 12
- homolog_centering_shift: float32 [256], replicated, may hold values from -3 to 3
- contact_scaling_factor: float32 [128], replicated, may hold values from 0.1 to 1.9
- asking_projection_matrix: bfloat16 [256, 256], replicated, may hold values from -0.375 to 0.375
- lookup_projection_matrix: bfloat16 [256, 256], replicated, may hold values from -0.375 to 0.375
- content_projection_matrix: bfloat16 [256, 256], replicated, may hold values from -0.375 to 0.375
- sigmoid_projection_matrix: bfloat16 [256, 256], replicated, may hold values from -0.375 to 0.375
- sigmoid_shift_term: float32 [256], replicated, may hold values from -4 to 4
- contact_logit_projection: bfloat16 [128, 8], replicated, may hold values from -0.5 to 0.5
- final_projection_matrix: bfloat16 [256, 256], replicated, may hold values from -0.375 to 0.375
Outputs:
- update: bfloat16 [160, 2048, 256], P('seq', 'res')
The draws below stay inside these ranges and needn't reach their ends.
All inputs are finite; a program needn't handle non-finite values.
Results may differ from the reference program's by a relative error of at most 0.0075.
The reference program's roundings to bfloat16 on the way count: a program that leaves them out, or rounds other values in their place, can miss the bound.
Values may be sent and summed in bfloat16 or wider, within the bound.
A program may use at most 128 MiB of HBM per device.

```python
import math
import jax
import jax.numpy as jnp
from jax import lax

CHANNEL_SIZE = 256
CP = 128
H = 8
HD = 32
HOMOLOG_TOTAL = 160
AMINO_TOTAL = 2048


def draw_homolog_scaling_factor(key, part):
    key = jax.random.fold_in(key, 11)
    upper = 2.0
    unit = jax.random.uniform(key, (CHANNEL_SIZE,), jnp.float32)
    return 0.5 * jnp.exp(unit * jnp.log(upper / 0.5))


def shard_levels(own_key, extent, pieces, smallest, top_value):
    level = 1.0
    for dim, blocks in pieces:
        draws = jax.random.uniform(jax.random.fold_in(jax.random.fold_in(own_key, 6), dim), (blocks,), jnp.float32, smallest / len(pieces), top_value / len(pieces))
        level = level * jnp.repeat(jnp.exp(draws), extent[dim] // blocks).reshape((-1,) + (1,) * (len(extent) - 1 - dim))
    return level


def centred(stream_key, extent, deviation, limit, cuts=(), dtype=jnp.bfloat16):
    loudness = shard_levels(stream_key, extent, cuts, -0.22, 0.18) if cuts else 1.0
    result = jax.random.normal(stream_key, extent, jnp.float32) * deviation * loudness
    return jnp.minimum(jnp.maximum(result, -limit), limit).astype(dtype)


def setup_inputs(seed: int = 0) -> dict:
    arg_keys = jax.random.split(jax.random.key(seed), 13)
    return {
        "homolog_embedding": centred(arg_keys[0], (HOMOLOG_TOTAL, AMINO_TOTAL, CHANNEL_SIZE), 1.0, 6.0, ((0, 16), (1, 16))),
        "contact_embedding": centred(arg_keys[1], (AMINO_TOTAL, AMINO_TOTAL, CP), 1.0, 6.0, ((0, 16), (1, 16))),
        "homolog_scaling_factor": draw_homolog_scaling_factor(jax.random.fold_in(arg_keys[12], 71), 0),
        "homolog_centering_shift": centred(arg_keys[3], (CHANNEL_SIZE,), 0.5, 3.0, (), jnp.float32),
        "contact_scaling_factor": jnp.clip(1.0 + 0.18 * jax.random.normal(arg_keys[4], (CP,), jnp.float32), 0.1, 1.9),
        "asking_projection_matrix": centred(arg_keys[5], (CHANNEL_SIZE, CHANNEL_SIZE), CHANNEL_SIZE ** -0.5, 0.375),
        "lookup_projection_matrix": centred(arg_keys[6], (CHANNEL_SIZE, CHANNEL_SIZE), CHANNEL_SIZE ** -0.5, 0.375),
        "content_projection_matrix": centred(arg_keys[7], (CHANNEL_SIZE, CHANNEL_SIZE), CHANNEL_SIZE ** -0.5, 0.375),
        "sigmoid_projection_matrix": centred(arg_keys[8], (CHANNEL_SIZE, CHANNEL_SIZE), CHANNEL_SIZE ** -0.5, 0.375),
        "sigmoid_shift_term": centred(arg_keys[9], (CHANNEL_SIZE,), 1.0, 4.0, (), jnp.float32),
        "contact_logit_projection": centred(arg_keys[10], (CP, H), CP ** -0.5, 0.5),
        "final_projection_matrix": centred(arg_keys[11], (CHANNEL_SIZE, CHANNEL_SIZE), CHANNEL_SIZE ** -0.5, 0.375),
    }


def standardize_channels(values, gain, shift):
    mean = lax.optimization_barrier(jnp.mean(values, axis=-1, keepdims=True))
    centered = values - mean
    var = lax.optimization_barrier(jnp.mean(centered * centered, axis=-1, keepdims=True))
    return centered * lax.rsqrt(var + 1e-05) * gain + shift

def reference(homolog_embedding, contact_embedding, homolog_scaling_factor, homolog_centering_shift, contact_scaling_factor, asking_projection_matrix, lookup_projection_matrix, content_projection_matrix, sigmoid_projection_matrix, sigmoid_shift_term, contact_logit_projection, final_projection_matrix):
    homolog_standardized = standardize_channels(homolog_embedding.astype(jnp.float32), homolog_scaling_factor, homolog_centering_shift).astype(jnp.bfloat16)
    flat = homolog_standardized.reshape(HOMOLOG_TOTAL * AMINO_TOTAL, CHANNEL_SIZE)
    query = (jnp.dot(flat, asking_projection_matrix, preferred_element_type=jnp.float32) * HD ** (-0.5)).astype(jnp.bfloat16).reshape(HOMOLOG_TOTAL, AMINO_TOTAL, H, HD)
    key = jnp.dot(flat, lookup_projection_matrix, preferred_element_type=jnp.float32).astype(jnp.bfloat16).reshape(HOMOLOG_TOTAL, AMINO_TOTAL, H, HD)
    value = jnp.dot(flat, content_projection_matrix, preferred_element_type=jnp.float32).astype(jnp.bfloat16).reshape(HOMOLOG_TOTAL, AMINO_TOTAL, H, HD)
    gate = jax.nn.sigmoid(jnp.dot(flat, sigmoid_projection_matrix, preferred_element_type=jnp.float32) + sigmoid_shift_term).reshape(HOMOLOG_TOTAL, AMINO_TOTAL, CHANNEL_SIZE)
    block_rows = math.gcd(AMINO_TOTAL, 128)

    def bias_block(rows):
        normed_pair = standardize_channels(rows.astype(jnp.float32), contact_scaling_factor, 0.0).astype(jnp.bfloat16)
        out = jnp.dot(normed_pair.reshape(-1, CP), contact_logit_projection, preferred_element_type=jnp.float32)
        return out.astype(jnp.bfloat16).reshape(block_rows, AMINO_TOTAL, H)
    blocks = lax.map(bias_block, contact_embedding.reshape(AMINO_TOTAL // block_rows, block_rows, AMINO_TOTAL, CP))
    bias = blocks.reshape(AMINO_TOTAL, AMINO_TOTAL, H).transpose(2, 0, 1).astype(jnp.float32)

    def one_sequence(items):
        qq, kk, vv = items
        scores = jnp.einsum('qhd,khd->hqk', qq.astype(jnp.float32), kk.astype(jnp.float32)) + bias
        top = lax.optimization_barrier(jnp.max(scores, axis=-1, keepdims=True))
        weights = jnp.exp(scores - top)
        total = lax.optimization_barrier(jnp.sum(weights, axis=-1))
        rounded = lax.optimization_barrier(weights.astype(jnp.bfloat16))
        out = jnp.einsum('hqk,khd->qhd', rounded.astype(jnp.float32), vv.astype(jnp.float32))
        out = out / total.T[:, :, None]
        return out.reshape(AMINO_TOTAL, CHANNEL_SIZE)
    attended = lax.map(one_sequence, (query, key, value))
    gated = (gate * attended).astype(jnp.bfloat16)
    update = jnp.dot(gated.reshape(HOMOLOG_TOTAL * AMINO_TOTAL, CHANNEL_SIZE), final_projection_matrix, preferred_element_type=jnp.float32)
    return update.astype(jnp.bfloat16).reshape(HOMOLOG_TOTAL, AMINO_TOTAL, CHANNEL_SIZE)
```

```python
import functools

import jax
import jax.numpy as jnp
from jax import lax
from jax.experimental import pallas as pl
from jax.experimental.pallas import tpu as pltpu
from jax.sharding import PartitionSpec as P

F32, BF = jnp.float32, jnp.bfloat16
MESH = pl.DeviceIdType.MESH
VMEM = pl.BlockSpec(memory_space=pltpu.VMEM)
HBM = pl.BlockSpec(memory_space=pl.ANY)

H, HD = 8, 32
SEQS, RES, CH, CP = 10, 128, 256, 128
KEYS = 2048
ROWS = SEQS * HD
PAIRS = SEQS // 2
TILE = 256
LIMIT = 56 * 2**20


def normalize(values, gain):
    mean = jnp.mean(values, axis=-1, keepdims=True)
    centered = values - mean
    var = jnp.mean(centered * centered, axis=-1, keepdims=True)
    return centered * lax.rsqrt(var + 1e-05) * gain


def pair_kernel(steps, x_ref, gain_ref, w_ref, o_ref, scr):
    step = pl.program_id(0)
    n = x_ref.shape[0]
    x = x_ref[...].reshape(n * RES, CP).astype(F32)
    pn = normalize(x, gain_ref[...]).astype(BF)
    out = lax.dot_general(w_ref[...], pn, (((1,), (1,)), ((), ())), preferred_element_type=F32)
    for i in range(n):
        row = pl.multiple_of((step * n + i) * H, H)
        scr[pl.ds(row, H), :] = out[:, i * RES : (i + 1) * RES]

    @pl.when(step == steps - 1)
    def _():
        for h in range(H):
            o_ref[h] = scr[pl.ds(h, RES, stride=H), :].T.astype(BF)


def pair_bias(contact, gain, w):
    n = 16
    steps = RES // n
    return pl.pallas_call(
        functools.partial(pair_kernel, steps),
        name="pair_bias",
        grid=(steps,),
        out_shape=jax.ShapeDtypeStruct((H, RES, RES), BF),
        in_specs=[
            pl.BlockSpec((n, RES, CP), lambda i: (i, 0, 0)),
            pl.BlockSpec((1, CP), lambda i: (0, 0)),
            pl.BlockSpec((H, CP), lambda i: (0, 0)),
        ],
        out_specs=pl.BlockSpec((H, RES, RES), lambda i: (0, 0, 0)),
        scratch_shapes=[pltpu.VMEM((RES * H, RES), F32)],
    )(contact, gain.reshape(1, CP), w.T)


def proj_kernel(x_ref, gain_ref, shift_ref, wk_ref, wv_ref, wq_ref, wg_ref, gs_ref, qkv_ref, gate_ref):
    wt = [w[...].astype(F32).T.astype(BF) for w in (wk_ref, wv_ref, wq_ref, wg_ref)]
    nt = (((1,), (1,)), ((), ()))
    for p in range(PAIRS):
        x = x_ref[2 * p : 2 * p + 2].reshape(2 * RES, CH).astype(F32)
        normed = (normalize(x, gain_ref[...]) + shift_ref[...]).astype(BF)
        for j in range(3):
            y = lax.dot_general(wt[j], normed, nt, preferred_element_type=F32)
            if j == 2:
                y = y * HD ** (-0.5)
            y = y.astype(BF)
            for h in range(H):
                for s in range(2):
                    qkv_ref[h, j, (2 * p + s) * HD : (2 * p + s + 1) * HD, :] = y[
                        h * HD : (h + 1) * HD, s * RES : (s + 1) * RES
                    ]
        g = jax.nn.sigmoid(
            lax.dot_general(wt[3], normed, nt, preferred_element_type=F32) + gs_ref[...]
        )
        gate_ref[2 * p] = g[:, :RES]
        gate_ref[2 * p + 1] = g[:, RES:]


def projections(x, gain, shift, wk, wv, wq, wg, gs):
    return pl.pallas_call(
        proj_kernel,
        name="projections",
        out_shape=(
            jax.ShapeDtypeStruct((H, 3, ROWS, RES), BF),
            jax.ShapeDtypeStruct((SEQS, CH, RES), F32),
        ),
        in_specs=[VMEM] * 8,
        out_specs=(VMEM, VMEM),
        compiler_params=pltpu.CompilerParams(vmem_limit_bytes=LIMIT),
    )(x, gain.reshape(1, CH), shift.reshape(1, CH), wk, wv, wq, wg, gs.reshape(CH, 1))


def aligned(value, n):
    return pl.multiple_of(value, n)


def attention_kernel(
    qkv, tiles, out,
    kt, vt, qt, bias, kn, sa, sb, o,
    tile_send, lo_send, kvq_send, core_send, ring_send, out_send,
    bias_recv, kvq_recv, core_recv, ring_recv, out_recv, local_sem,
):
    seq, res = lax.axis_index("seq"), lax.axis_index("res")
    z, low = seq // 2, lax.rem(seq, 2)
    chip, core = res // 2, lax.rem(res, 2)
    owner = core == low

    def at(other_chip, other_core):
        return (seq, other_chip * 2 + other_core)

    def along_z(d):
        return (lax.rem(z + d + 8, 8) * 2 + low, res)

    sibling = at(chip, 1 - core)
    across = (z * 2 + 1 - low, res)

    def remote(src, dst, send, recv, device):
        return pltpu.make_async_remote_copy(
            src_ref=src, dst_ref=dst, send_sem=send, recv_sem=recv, device_id=device, device_id_type=MESH
        )

    def wait_bytes(ref, sem):
        pltpu.make_async_copy(ref, ref, sem).wait()

    barrier = pltpu.get_barrier_semaphore()
    for d in range(1, 16):
        pl.semaphore_signal(barrier, inc=1, device_id=(seq, lax.rem(res + d, 16)), device_id_type=MESH)
    for peer in (across, along_z(1), along_z(-1)):
        pl.semaphore_signal(barrier, inc=1, device_id=peer, device_id_type=MESH)
    pl.semaphore_wait(barrier, 18)

    mine = pl.ds(aligned(core * 1024 + chip * RES, RES), RES)

    def tile_copy(d):
        to = lax.rem(chip + d, 8)
        return remote(tiles.at[to], bias.at[z, mine, :], tile_send.at[d], bias_recv, at(to, low))

    tile_local = pltpu.make_async_copy(tiles.at[chip], bias.at[z, mine, :], bias_recv)
    for d in range(1, 8):
        tile_copy(d).start()

    @pl.when(owner)
    def _():
        tile_local.start()

    @pl.when(jnp.logical_not(owner))
    def _():
        tile_copy(0).start()

    def kvq_copies(d):
        to = lax.rem(chip + d, 8)
        dsts = (kt.at[:, mine], vt.at[:, mine], qt.at[chip])
        return [
            remote(qkv.at[to, j], dsts[j], kvq_send.at[d, j], kvq_recv.at[j], at(to, core)) for j in range(3)
        ]

    for j, dst in enumerate((kt.at[:, mine], vt.at[:, mine], qt.at[chip])):
        pltpu.make_async_copy(qkv.at[chip, j], dst, kvq_recv.at[j]).start()
    for d in range(1, 8):
        for c in kvq_copies(d):
            c.start()

    def ring_copy(sign, k):
        chunk = lax.rem(z - sign * (k - 1) + 8, 8)
        ref = bias.at[chunk]
        if k == 4:
            ref = bias.at[chunk, pl.ds(0 if sign > 0 else KEYS // 2, KEYS // 2), :]
        i = 0 if sign > 0 else 1
        return remote(ref, ref, ring_send.at[i, k - 1], ring_recv.at[i, k - 1], along_z(sign))

    def ring_arrived(sign, k):
        chunk = lax.rem(z - sign * k + 8, 8)
        ref = bias.at[chunk]
        if k == 4:
            ref = bias.at[chunk, pl.ds(0 if sign > 0 else KEYS // 2, KEYS // 2), :]
        wait_bytes(ref, ring_recv.at[0 if sign > 0 else 1, k - 1])

    wait_bytes(bias.at[z], bias_recv)
    lo_copy = remote(bias.at[z], bias.at[z], lo_send, bias_recv, across)

    @pl.when(owner)
    def _():
        lo_copy.start()

    ring_copy(1, 1).start()
    ring_copy(-1, 1).start()

    ring_arrived(1, 1)
    ring_copy(1, 2).start()
    ring_arrived(-1, 1)
    ring_copy(-1, 2).start()

    here = pl.ds(aligned(core * 1024, 1024), 1024)
    there = pl.ds(aligned((1 - core) * 1024, 1024), 1024)
    passed = []
    for j, ref in enumerate((kt, vt)):
        wait_bytes(ref.at[:, here], kvq_recv.at[j])
        c = remote(ref.at[:, here], ref.at[:, here], core_send.at[j], core_recv.at[j], sibling)
        c.start()
        passed.append(c)

    def turn_keys(half):
        for b in range(8):
            rows = pl.ds(aligned(half * 1024 + b * RES, RES), RES)
            block = kt[:, rows].astype(F32)
            for p in range(PAIRS):
                kn[p, rows, :] = block[p * 2 * HD : (p + 1) * 2 * HD].T.astype(BF)

    turn_keys(core)
    wait_bytes(kt.at[:, there], core_recv.at[0])
    turn_keys(1 - core)
    wait_bytes(vt.at[:, there], core_recv.at[1])
    wait_bytes(qt, kvq_recv.at[2])

    def chunk_of(k):
        far = jnp.where(lax.rem(k, 2) == 1, -((k + 1) // 2), k // 2)
        return lax.rem(z + far + 8, 8)

    def before(k):
        for i in range(1, 8):
            sign, hop = (1, (i + 1) // 2) if i % 2 else (-1, i // 2)

            if i < 3:
                continue

            @pl.when(k == i)
            def _(sign=sign, hop=hop):
                ring_arrived(sign, hop)
                if hop < 4:
                    ring_copy(sign, hop + 1).start()
                else:
                    ring_arrived(-1, 4)

    def out_copy(k):
        to = chunk_of(k)
        return to, remote(o.at[k], out.at[chip], out_send.at[k], out_recv.at[chip], at(to, core))

    def after(k):
        to, copy = out_copy(k)

        @pl.when(to != chip)
        def _():
            copy.start()

        @pl.when(to == chip)
        def _():
            pltpu.make_async_copy(o.at[k], out.at[chip], out_recv.at[chip]).start()

    def rhs_of(chunk, p):
        q = qt[chunk, pl.ds(aligned(p * 64, 64), 64), :]
        none = jnp.zeros((HD, RES), BF)
        return jnp.concatenate(
            [jnp.concatenate([q[:HD], none], 1), jnp.concatenate([none, q[HD:]], 1)], 0
        )

    def score_tile(t, rhs, p, chunk, s, top):
        rows = pl.ds(t * TILE, TILE)
        b = bias[chunk, rows, :].astype(F32)
        scores = jnp.dot(kn[p, rows, :], rhs, preferred_element_type=F32) + jnp.concatenate([b, b], 1)
        s[rows, :] = scores
        return jnp.maximum(top, jnp.max(scores.reshape(TILE // 8, 8, 2 * RES), axis=0))

    def value_tile(t, p, s, top, total, acc):
        rows = pl.ds(t * TILE, TILE)
        e = jnp.exp(s[rows, :] - top)
        total = total + jnp.sum(e.reshape(TILE // 8, 8, 2 * RES), axis=0)
        v = vt[pl.ds(aligned(p * 64, 64), 64), rows]
        return total, acc + jnp.dot(v, e.astype(BF), preferred_element_type=F32)

    lowest = jnp.full((8, 2 * RES), -jnp.inf, F32)
    tiles_n = KEYS // TILE

    def first(s):
        chunk = chunk_of(jnp.int32(0))
        rhs = rhs_of(chunk, jnp.int32(0))
        top = lowest
        for t in range(tiles_n):
            top = score_tile(t, rhs, jnp.int32(0), chunk, s, top)
        return top

    def both(u, v, top, s_now, s_next):
        k, p = u // PAIRS, lax.rem(u, PAIRS)
        kv, pv = v // PAIRS, lax.rem(v, PAIRS)
        chunk = chunk_of(kv)

        @pl.when(jnp.logical_and(pv == 0, v < 8 * PAIRS))
        def _():
            before(kv)

        kv = jnp.minimum(kv, 7)
        chunk = chunk_of(kv)
        top = jnp.max(top, axis=0, keepdims=True)
        rhs = rhs_of(chunk, pv)
        total = jnp.zeros((8, 2 * RES), F32)
        acc = jnp.zeros((2 * HD, 2 * RES), F32)
        top_next = lowest
        for t in range(tiles_n):
            top_next = score_tile(t, rhs, pv, chunk, s_next, top_next)
            total, acc = value_tile(t, p, s_now, top, total, acc)
        result = acc / jnp.sum(total, axis=0, keepdims=True)
        o[k, pl.ds(aligned(p * 64, 64), HD), :] = result[:HD, :RES]
        o[k, pl.ds(aligned(p * 64 + HD, HD), HD), :] = result[HD:, RES:]

        @pl.when(p == PAIRS - 1)
        def _():
            after(k)

        return top_next

    def body(i, top):
        top = both(2 * i, 2 * i + 1, top, sa, sb)
        return both(2 * i + 1, 2 * i + 2, top, sb, sa)

    lax.fori_loop(0, 4 * PAIRS, body, first(sa))

    for h in range(8):
        wait_bytes(out.at[h], out_recv.at[h])
    for k in range(8):
        to, copy = out_copy(jnp.int32(k))

        @pl.when(to != chip)
        def _(copy=copy):
            copy.wait_send()

    for d in range(1, 8):
        tile_copy(d).wait_send()
        for c in kvq_copies(d):
            c.wait_send()

    @pl.when(jnp.logical_not(owner))
    def _():
        tile_copy(0).wait_send()

    @pl.when(owner)
    def _():
        lo_copy.wait_send()

    for c in passed:
        c.wait_send()
    for k in range(1, 5):
        ring_copy(1, k).wait_send()
        ring_copy(-1, k).wait_send()


def attention(qkv, tiles):
    dma = pltpu.SemaphoreType.DMA
    return pl.pallas_call(
        attention_kernel,
        name="attention",
        out_shape=jax.ShapeDtypeStruct((H, ROWS, RES), F32),
        in_specs=[VMEM, VMEM],
        out_specs=VMEM,
        scratch_shapes=[
            pltpu.VMEM((ROWS, KEYS), BF),
            pltpu.VMEM((ROWS, KEYS), BF),
            pltpu.VMEM((8, ROWS, RES), BF),
            pltpu.VMEM((8, KEYS, RES), BF),
            pltpu.VMEM((PAIRS, KEYS, 2 * HD), BF),
            pltpu.VMEM((KEYS, 2 * RES), F32),
            pltpu.VMEM((KEYS, 2 * RES), F32),
            pltpu.VMEM((8, ROWS, RES), F32),
            dma((8,)),
            dma,
            dma((8, 3)),
            dma((2,)),
            dma((2, 4)),
            dma((8,)),
            dma,
            dma((3,)),
            dma((2,)),
            dma((2, 4)),
            dma((8,)),
            dma,
        ],
        compiler_params=pltpu.CompilerParams(
            collective_id=0, has_side_effects=True, vmem_limit_bytes=LIMIT
        ),
    )(qkv, tiles)


def final_kernel(a_ref, gate_ref, w_ref, o_ref):
    w = w_ref[...]
    for s in range(SEQS):
        attended = jnp.concatenate([a_ref[h, s * HD : (s + 1) * HD, :] for h in range(H)], 0)
        gated = (gate_ref[s] * attended).T.astype(BF)
        o_ref[s] = jnp.dot(gated, w, preferred_element_type=F32).astype(BF)


def final(attended, gate, w):
    return pl.pallas_call(
        final_kernel,
        name="final",
        out_shape=jax.ShapeDtypeStruct((SEQS, RES, CH), BF),
        in_specs=[VMEM] * 3,
        out_specs=VMEM,
        compiler_params=pltpu.CompilerParams(vmem_limit_bytes=LIMIT),
    )(attended, gate, w)


def local(x, pair, x_gain, x_shift, pair_gain, wq, wk, wv, wg, gate_shift, w_bias, w_out):
    tiles = pair_bias(pair, pair_gain, w_bias)
    qkv, gate = projections(x, x_gain, x_shift, wk, wv, wq, wg, gate_shift)
    return final(attention(qkv, tiles), gate, w_out)


def solution(mesh):
    split = P("seq", "res", None)
    in_specs = (split, split) + (P(),) * 10
    return jax.shard_map(local, mesh=mesh, in_specs=in_specs, out_specs=split, check_vma=False)
```

```python
import jax
import jax.numpy as jnp
from jax import lax
from jax.experimental import pallas as pl
from jax.experimental.pallas import tpu as pltpu
from jax.sharding import PartitionSpec as P

F32, BF = jnp.float32, jnp.bfloat16
MESH = pl.DeviceIdType.MESH
VMEM = pl.BlockSpec(memory_space=pltpu.VMEM)
HBM = pl.BlockSpec(memory_space=pl.ANY)

H, HD = 8, 32
SEQS, RES, CH, CP = 10, 128, 256, 128
KEYS = 2048
ROWS = SEQS * HD
PAIRS = SEQS // 2
PW = 2 * HD
TILE = 256
STEP = 32
LIMIT = 60 * 2**20
RING_AT = ((1, 1, 0), (2, 1, 1), (9, 2, 0), (12, 2, 1), (20, 3, 0), (25, 3, 1), (35, 4, 0))
SEND_AT = {}
GATE_AT = 15
MIDDLE = 2
EARLY = 1


def aligned(value, n):
    return pl.multiple_of(value, n)


def column(row, n):
    return jnp.broadcast_to(row, (n, row.shape[1])).T


def normalize(values, gain):
    mean = jnp.mean(values, axis=0, keepdims=True)
    centered = values - mean
    var = jnp.mean(centered * centered, axis=0, keepdims=True)
    return centered * lax.rsqrt(var + 1e-05) * gain


def kernel(
    x_hbm, pair_hbm, gain_ref, shift_ref, pair_gain_ref, wq_hbm, wk_hbm, wv_hbm, wg_hbm, gs_ref, wb_ref, wo_hbm,
    out,
    pair_v, x_v, w_v, logits, tiles, normed_v, qkv, gate, gate_in, came, bias, kn, sa, sb, o, o_last, back, gated_v,
    pair_in, x_in, w_in,
    tile_send, qkv_send, gate_send, core_send, ring_send, back_send, last_send,
    bias_recv, qkv_recv, gate_recv, core_recv, ring_recv, back_recv, last_recv,
):
    seq, res = lax.axis_index("seq"), lax.axis_index("res")
    z, low = seq // 2, lax.rem(seq, 2)
    chip, core = res // 2, lax.rem(res, 2)
    owner = core == low

    pair_copies = [
        pltpu.make_async_copy(pair_hbm.at[pl.ds(i * STEP, STEP)], pair_v.at[pl.ds(i * STEP, STEP)], pair_in.at[i])
        for i in range(RES // STEP)
    ]
    for c in pair_copies:
        c.start()
    x_copy = pltpu.make_async_copy(x_hbm, x_v, x_in)
    x_copy.start()
    w_copies = [
        pltpu.make_async_copy(w, w_v.at[i], w_in.at[i])
        for i, w in enumerate((wk_hbm, wv_hbm, wq_hbm, wg_hbm, wo_hbm))
    ]
    for c in w_copies:
        c.start()

    def at(other_chip, other_core):
        return (seq, other_chip * 2 + other_core)

    def along_z(d):
        return (lax.rem(z + d + 8, 8) * 2 + low, res)

    sibling = at(chip, 1 - core)

    def remote(src, dst, send, recv, device):
        return pltpu.make_async_remote_copy(
            src_ref=src, dst_ref=dst, send_sem=send, recv_sem=recv, device_id=device, device_id_type=MESH
        )

    def wait_bytes(ref, sem):
        pltpu.make_async_copy(ref, ref, sem).wait()

    barrier = pltpu.get_barrier_semaphore()
    for other in range(2):
        for d in range(other ^ 1, 16):
            peer = (z * 2 + lax.rem(low + other, 2), lax.rem(res + d, 16))
            pl.semaphore_signal(barrier, inc=1, device_id=peer, device_id_type=MESH)
    for sign in (1, -1):
        pl.semaphore_signal(barrier, inc=1, device_id=along_z(sign), device_id_type=MESH)

    def qkv_copy(d, p):
        to = lax.rem(chip + d, 8)
        return remote(qkv.at[to, p], came.at[p, core, chip], qkv_send.at[p, d], qkv_recv.at[p], at(to, core))

    x_gain, x_shift = column(gain_ref[...], 2 * RES), column(shift_ref[...], 2 * RES)
    x_copy.wait()
    for c in w_copies:
        c.wait()
    wt = [w_v[i].astype(F32).T.astype(BF) for i in range(4)]

    def project(p):
        turned = jnp.concatenate([x_v[2 * p].T, x_v[2 * p + 1].T], 1).astype(F32)
        normed = (normalize(turned, x_gain) + x_shift).astype(BF)
        normed_v[p] = normed
        for j in range(3):
            y = jnp.dot(wt[j], normed, preferred_element_type=F32)
            if j == 2:
                y = y * HD ** (-0.5)
            y = y.astype(BF)
            for h in range(H):
                for s in range(2):
                    qkv[h, p, j, s * HD : (s + 1) * HD, :] = y[h * HD : (h + 1) * HD, s * RES : (s + 1) * RES]

    def send_pair(p):
        pltpu.make_async_copy(qkv.at[chip, p], came.at[p, core, chip], qkv_recv.at[p]).start()
        for d in range(1, 8):
            qkv_copy(d, p).start()

    pl.semaphore_wait(barrier, 33)
    for p in range(EARLY):
        project(p)
        send_pair(p)

    pair_gain = column(pair_gain_ref[...], RES)
    pair_gain = jnp.concatenate([pair_gain, pair_gain], 1)
    wb = wb_ref[...]

    def pair_step(i, carry):
        rows = pl.ds(i * STEP, STEP)
        pltpu.make_async_copy(pair_hbm.at[rows], pair_v.at[rows], pair_in.at[i]).wait()
        for j in range(STEP // 2):
            row = i * STEP + 2 * j
            turned = jnp.concatenate([pair_v[row].T, pair_v[row + 1].T], 1).astype(F32)
            y = jnp.dot(wb, normalize(turned, pair_gain).astype(BF), preferred_element_type=F32)
            row = aligned(row * H, 2 * H)
            logits[pl.ds(row, H), :] = y[:, :RES]
            logits[pl.ds(row + H, H), :] = y[:, RES:]
        return carry

    lax.fori_loop(0, RES // STEP, pair_step, 0)
    for h in range(H):
        tiles[h] = logits[pl.ds(h, RES, stride=H), :].T.astype(BF)

    mine = pl.ds(aligned(core * 1024 + chip * RES, RES), RES)

    def tile_copy(d, other):
        to = lax.rem(chip + d, 8)
        device = (z * 2 + lax.rem(low + other, 2), to * 2 + low)
        return remote(tiles.at[to], bias.at[z, mine, :], tile_send.at[other, d], bias_recv, device)

    @pl.when(owner)
    def _():
        pltpu.make_async_copy(tiles.at[chip], bias.at[z, mine, :], bias_recv).start()

    @pl.when(jnp.logical_not(owner))
    def _():
        tile_copy(0, 0).start()

    tile_copy(0, 1).start()
    for d in range(1, 8):
        for other in range(2):
            tile_copy(d, other).start()

    def half_of(chunk, half):
        return bias.at[chunk, pl.ds(half * (KEYS // 2), KEYS // 2), :]

    def ring_copy(sign, k, half):
        i = 0 if sign > 0 else 1
        ref = half_of(lax.rem(z - sign * (k - 1) + 8, 8), half)
        return remote(ref, ref, ring_send.at[i, k - 1, half], ring_recv.at[i, k - 1, half], along_z(sign))

    def ring_arrived(sign, k, half):
        ref = half_of(lax.rem(z - sign * k + 8, 8), half)
        wait_bytes(ref, ring_recv.at[0 if sign > 0 else 1, k - 1, half])

    def goes(sign, k, half):
        return k < 4 or (k == 4 and half == (0 if sign > 0 else 1))

    def take(sign, k, half):
        if goes(sign, k, half):
            ring_arrived(sign, k, half)
        if goes(sign, k + 1, half):
            ring_copy(sign, k + 1, half).start()

    for p in range(EARLY, PAIRS):
        project(p)
        if p == MIDDLE:
            wait_bytes(bias.at[z], bias_recv)
            for half in range(2):
                for sign in (1, -1):
                    ring_copy(sign, 1, half).start()
        if p not in SEND_AT.values():
            send_pair(p)

    gate_shift = column(gs_ref[...], 2 * RES)
    for p in range(PAIRS):
        g = jax.nn.sigmoid(jnp.dot(wt[3], normed_v[p], preferred_element_type=F32) + gate_shift)
        for h in range(H):
            for s in range(2):
                gate[h, (2 * p + s) * HD : (2 * p + s + 1) * HD, :] = g[
                    h * HD : (h + 1) * HD, s * RES : (s + 1) * RES
                ]

    last = lax.rem(z + 4, 8)

    def gate_copy(d):
        to = lax.rem(chip + d, 8)
        return remote(gate.at[to], gate_in, gate_send.at[d], gate_recv, at(to, core))

    def send_gate():
        pltpu.make_async_copy(gate.at[chip], gate_in, gate_recv).start()
        for d in range(1, 8):
            gate_copy(d).start()

    def core_copy(p):
        ref = came.at[p, core, :, pl.ds(0, 2)]
        return remote(ref, ref, core_send.at[p], core_recv.at[p], sibling)

    def turn_keys(p, half):
        for b in range(8):
            rows = pl.ds(aligned(half * 1024 + b * RES, RES), RES)
            kn[p, rows, :] = came[p, half, b, 0].astype(F32).T.astype(BF)

    def pair_arrived(p):
        wait_bytes(came.at[p, core], qkv_recv.at[p])
        core_copy(p).start()
        turn_keys(p, core)
        wait_bytes(came.at[p, 1 - core, :, pl.ds(0, 2)], core_recv.at[p])
        turn_keys(p, 1 - core)

    def chunk_of(k):
        far = jnp.where(lax.rem(k, 2) == 1, -((k + 1) // 2), k // 2)
        return lax.rem(z + far + 8, 8)

    def place(v):
        w = v - 15
        k = jnp.where(v < 9, v // 3, jnp.where(v < 15, lax.rem(v, 3), 3 + w // PAIRS))
        p = jnp.where(v < 9, lax.rem(v, 3), jnp.where(v < 15, v // 3, lax.rem(v, PAIRS)))
        return k, p

    def before(v):
        k, p = place(v)

        for unit, hop, half in RING_AT:

            @pl.when(v == unit)
            def _(hop=hop, half=half):
                for sign in (1, -1):
                    take(sign, hop, half)
                    if hop == 4:
                        take(sign, hop, 1)

        @pl.when(jnp.logical_and(v == GATE_AT, chip == last))
        def _():
            send_gate()

        @pl.when(jnp.logical_and(k == 0, v < 15))
        def _():
            pair_arrived(p)

        for unit, pair in SEND_AT.items():

            @pl.when(v == unit)
            def _(pair=pair):
                send_pair(pair)

    def after(k, p):
        to = chunk_of(k)
        rows = pl.ds(aligned(p * PW, PW), PW)

        def send(src, dst, send_sem, recv_sem):
            @pl.when(to != chip)
            def _():
                remote(src, dst, send_sem, recv_sem, at(to, core)).start()

            @pl.when(to == chip)
            def _():
                pltpu.make_async_copy(src, dst, recv_sem).start()

        @pl.when(k < 7)
        def _():
            send(o.at[k, rows, :], back.at[chip, rows, :], back_send, back_recv)

        @pl.when(k == 7)
        def _():
            send(o_last.at[rows, :], gated_v.at[chip, rows, :], last_send, last_recv)

    def rhs_of(chunk, p):
        q = came[p, core, chunk, 2]
        none = jnp.zeros((HD, RES), BF)
        return jnp.concatenate([jnp.concatenate([q[:HD], none], 1), jnp.concatenate([none, q[HD:]], 1)], 0)

    def score_tile(t, rhs, p, chunk, s, top):
        rows = pl.ds(t * TILE, TILE)
        b = bias[chunk, rows, :].astype(F32)
        scores = jnp.dot(kn[p, rows, :], rhs, preferred_element_type=F32) + jnp.concatenate([b, b], 1)
        s[rows, :] = scores
        return jnp.maximum(top, jnp.max(scores.reshape(TILE // 8, 8, 2 * RES), axis=0))

    def value_tile(t, p, s, top, total, acc):
        e = jnp.exp(s[pl.ds(t * TILE, TILE), :] - top)
        total = total + jnp.sum(e.reshape(TILE // 8, 8, 2 * RES), axis=0)
        v = [came[p, (t * TILE) // 1024, (t * TILE) % 1024 // RES + i, 1] for i in range(TILE // RES)]
        return total, acc + jnp.dot(jnp.concatenate(v, 1), e.astype(BF), preferred_element_type=F32)

    lowest = jnp.full((8, 2 * RES), -jnp.inf, F32)
    steps = KEYS // TILE
    units = 8 * PAIRS

    def first(s):
        zero = jnp.int32(0)
        before(zero)
        rhs = rhs_of(z, zero)
        top = lowest
        for t in range(steps):
            top = score_tile(t, rhs, zero, z, s, top)
        return top

    def both(u, top, s_now, s_next):
        before(u + 1)
        k, p = place(u)
        kv, pv = place(jnp.minimum(u + 1, units - 1))
        chunk = chunk_of(kv)
        top = jnp.max(top, axis=0, keepdims=True)
        rhs = rhs_of(chunk, pv)
        total = jnp.zeros((8, 2 * RES), F32)
        acc = jnp.zeros((PW, 2 * RES), F32)
        top_next = lowest
        for t in range(steps):
            top_next = score_tile(t, rhs, pv, chunk, s_next, top_next)
            total, acc = value_tile(t, p, s_now, top, total, acc)
        result = acc / jnp.sum(total, axis=0, keepdims=True)
        halves = (result[:HD, :RES], result[HD:, RES:])

        @pl.when(k < 7)
        def _():
            for i, half in enumerate(halves):
                o[k, pl.ds(aligned(p * PW + i * HD, HD), HD), :] = half

        @pl.when(k == 7)
        def _():
            @pl.when(p == 0)
            def _():
                wait_bytes(gate_in, gate_recv)

            for i, half in enumerate(halves):
                rows = pl.ds(aligned(p * PW + i * HD, HD), HD)
                o_last[rows, :] = (gate_in[rows, :] * half).astype(BF)

        after(k, p)
        return top_next

    def body(i, top):
        top = both(2 * i, top, sa, sb)
        return both(2 * i + 1, top, sb, sa)

    lax.fori_loop(0, units // 2, body, first(sa))

    @pl.when(chip != last)
    def _():
        wait_bytes(back, back_recv)
        for h in range(H):
            gated_v[h] = (gate[h] * back[h]).astype(BF)

    @pl.when(chip == last)
    def _():
        wait_bytes(gated_v, last_recv)

    wo = w_v[4]
    for s in range(SEQS):
        gated = jnp.concatenate([gated_v[h, s * HD : (s + 1) * HD, :] for h in range(H)], 0)
        out[s] = jnp.dot(gated.T, wo, preferred_element_type=F32).astype(BF)

    @pl.when(chip != last)
    def _():
        wait_bytes(o.at[pl.ds(0, 6)], back_send)
        wait_bytes(o_last, last_send)

    @pl.when(chip == last)
    def _():
        wait_bytes(o.at[pl.ds(0, 7)], back_send)
        for d in range(1, 8):
            gate_copy(d).wait_send()
    for d in range(8):
        tile_copy(d, 1).wait_send()
        if d:
            tile_copy(d, 0).wait_send()

    @pl.when(jnp.logical_not(owner))
    def _():
        tile_copy(0, 0).wait_send()

    for p in range(PAIRS):
        for d in range(1, 8):
            qkv_copy(d, p).wait_send()
        core_copy(p).wait_send()
    for sign in (1, -1):
        for half in range(2):
            for k in range(1, 5):
                if goes(sign, k, half):
                    ring_copy(sign, k, half).wait_send()


def local(x, pair, x_gain, x_shift, pair_gain, wq, wk, wv, wg, gate_shift, w_bias, w_out):
    dma = pltpu.SemaphoreType.DMA
    return pl.pallas_call(
        kernel,
        name="attention",
        out_shape=jax.ShapeDtypeStruct((SEQS, RES, CH), BF),
        in_specs=[HBM, HBM, VMEM, VMEM, VMEM, HBM, HBM, HBM, HBM, VMEM, VMEM, HBM],
        out_specs=VMEM,
        scratch_shapes=[
            pltpu.VMEM((RES, RES, CP), BF),
            pltpu.VMEM((SEQS, RES, CH), BF),
            pltpu.VMEM((5, CH, CH), BF),
            pltpu.VMEM((RES * H, RES), F32),
            pltpu.VMEM((H, RES, RES), BF),
            pltpu.VMEM((PAIRS, CH, 2 * RES), BF),
            pltpu.VMEM((H, PAIRS, 3, PW, RES), BF),
            pltpu.VMEM((H, ROWS, RES), F32),
            pltpu.VMEM((ROWS, RES), F32),
            pltpu.VMEM((PAIRS, 2, 8, 3, PW, RES), BF),
            pltpu.VMEM((8, KEYS, RES), BF),
            pltpu.VMEM((PAIRS, KEYS, PW), BF),
            pltpu.VMEM((KEYS, 2 * RES), F32),
            pltpu.VMEM((KEYS, 2 * RES), F32),
            pltpu.VMEM((7, ROWS, RES), F32),
            pltpu.VMEM((ROWS, RES), BF),
            pltpu.VMEM((8, ROWS, RES), F32),
            pltpu.VMEM((8, ROWS, RES), BF),
            dma((RES // STEP,)),
            dma,
            dma((5,)),
            dma((2, 8)),
            dma((PAIRS, 8)),
            dma((8,)),
            dma((PAIRS,)),
            dma((2, 4, 2)),
            dma,
            dma,
            dma,
            dma((PAIRS,)),
            dma,
            dma((PAIRS,)),
            dma((2, 4, 2)),
            dma,
            dma,
        ],
        compiler_params=pltpu.CompilerParams(
            collective_id=0, has_side_effects=True, vmem_limit_bytes=LIMIT
        ),
    )(
        x, pair, x_gain.reshape(1, CH), x_shift.reshape(1, CH), pair_gain.reshape(1, CP),
        wq, wk, wv, wg, gate_shift.reshape(1, CH), w_bias.T, w_out,
    )


def solution(mesh):
    split = P("seq", "res", None)
    in_specs = (split, split) + (P(),) * 10
    return jax.shard_map(local, mesh=mesh, in_specs=in_specs, out_specs=split, check_vma=False)
```

```python
import jax
import jax.numpy as jnp
from jax import lax
from jax.experimental import pallas as pl
from jax.experimental.pallas import tpu as pltpu
from jax.sharding import PartitionSpec as P

F32, BF = jnp.float32, jnp.bfloat16
MESH = pl.DeviceIdType.MESH
VMEM = pl.BlockSpec(memory_space=pltpu.VMEM)
HBM = pl.BlockSpec(memory_space=pl.ANY)

H, HD = 8, 32
SEQS, RES, CH, CP = 10, 128, 256, 128
KEYS = 2048
ROWS = SEQS * HD
PAIRS = SEQS // 2
PW = 2 * HD
TILE = 256
HALF = RES // 2
STEP = 16
LIMIT = 60 * 2**20
RING_AT = ((1, 1, 0), (2, 1, 1), (9, 2, 0), (12, 2, 1), (20, 3, 0), (25, 3, 1), (35, 4, 0))
SEND_AT = {}
GATE_AT = 9
START_AT = (0, 1)


def aligned(value, n):
    return pl.multiple_of(value, n)


def column(row, n):
    return jnp.broadcast_to(row, (n, row.shape[1])).T


def normalize(values, gain):
    mean = jnp.mean(values, axis=0, keepdims=True)
    centered = values - mean
    var = jnp.mean(centered * centered, axis=0, keepdims=True)
    return centered * lax.rsqrt(var + 1e-05) * gain


def kernel(
    x_hbm, pair_hbm, gain_ref, shift_ref, pair_gain_ref, wq_hbm, wk_hbm, wv_hbm, wg_hbm, gs_ref, wb_ref, wo_hbm,
    out,
    pair_v, x_v, w_v, logits, tiles, normed_v, qkv, gate, gate_in, came, bias, kn, sa, sb, o, o_last, back, gated_v,
    pair_in, x_in, w_in,
    tile_send, qkv_send, gate_send, core_send, ring_send, back_send, last_send,
    bias_recv, qkv_recv, gate_recv, core_recv, ring_recv, back_recv, last_recv,
):
    seq, res = lax.axis_index("seq"), lax.axis_index("res")
    z, low = seq // 2, lax.rem(seq, 2)
    chip, core = res // 2, lax.rem(res, 2)
    owner = core == low

    def pair_copy(half, i):
        rows, keys = pl.ds(i * STEP, STEP), pl.ds(half * HALF, HALF)
        return pltpu.make_async_copy(pair_hbm.at[rows, keys], pair_v.at[rows, keys], pair_in.at[half, i])

    for half in range(2):
        for i in range(RES // STEP):
            pair_copy(half, i).start()
    x_copy = pltpu.make_async_copy(x_hbm, x_v, x_in)
    x_copy.start()
    w_copies = [
        pltpu.make_async_copy(w, w_v.at[i], w_in.at[i])
        for i, w in enumerate((wk_hbm, wv_hbm, wq_hbm, wg_hbm, wo_hbm))
    ]
    for c in w_copies:
        c.start()

    def at(other_chip, other_core):
        return (seq, other_chip * 2 + other_core)

    def along_z(d):
        return (lax.rem(z + d + 8, 8) * 2 + low, res)

    sibling = at(chip, 1 - core)

    def remote(src, dst, send, recv, device):
        return pltpu.make_async_remote_copy(
            src_ref=src, dst_ref=dst, send_sem=send, recv_sem=recv, device_id=device, device_id_type=MESH
        )

    def wait_bytes(ref, sem):
        pltpu.make_async_copy(ref, ref, sem).wait()

    barrier = pltpu.get_barrier_semaphore()
    for other in range(2):
        for d in range(other ^ 1, 16):
            peer = (z * 2 + lax.rem(low + other, 2), lax.rem(res + d, 16))
            pl.semaphore_signal(barrier, inc=1, device_id=peer, device_id_type=MESH)
    for sign in (1, -1):
        pl.semaphore_signal(barrier, inc=1, device_id=along_z(sign), device_id_type=MESH)

    pair_gain = column(pair_gain_ref[...], RES)
    pair_gain = jnp.concatenate([pair_gain, pair_gain], 1)
    wb = wb_ref[...]

    mine = pl.ds(aligned((core * 8 + chip) * HALF, HALF), HALF)

    def logits_of(half):
        keys = slice(half * HALF, (half + 1) * HALF)

        def pair_step(i, carry):
            pair_copy(half, i).wait()
            pair_copy(half, i + RES // STEP // 2).wait()
            for j in range(STEP // 2):
                row = i * STEP + 2 * j
                blocks = [
                    jnp.concatenate([pair_v[row + k, keys, :], pair_v[row + k + HALF, keys, :]], 0).T
                    for k in range(2)
                ]
                turned = jnp.concatenate(blocks, 1).astype(F32)
                y = jnp.dot(wb, normalize(turned, pair_gain).astype(BF), preferred_element_type=F32)
                at_row = aligned(row * H, 2 * H)
                logits[pl.ds(at_row, H), :] = y[:, :RES]
                logits[pl.ds(at_row + H, H), :] = y[:, RES:]
            return carry

        lax.fori_loop(0, RES // STEP // 2, pair_step, 0)
        for h in range(H):
            t = logits[pl.ds(h, HALF, stride=H), :].T
            tiles[half, h] = jnp.concatenate([t[:HALF], t[HALF:]], 1).astype(BF)

    def tile_copy(half, d, other):
        to = lax.rem(chip + d, 8)
        device = (z * 2 + lax.rem(low + other, 2), to * 2 + low)
        return remote(
            tiles.at[half, to], bias.at[z, half, mine, :], tile_send.at[half, other, d], bias_recv.at[half], device
        )

    def send_tiles(half):
        @pl.when(owner)
        def _():
            pltpu.make_async_copy(tiles.at[half, chip], bias.at[z, half, mine, :], bias_recv.at[half]).start()

        @pl.when(jnp.logical_not(owner))
        def _():
            tile_copy(half, 0, 0).start()

        tile_copy(half, 0, 1).start()
        for d in range(1, 8):
            for other in range(2):
                tile_copy(half, d, other).start()

    logits_of(0)
    pl.semaphore_wait(barrier, 33)
    send_tiles(0)
    logits_of(1)
    send_tiles(1)

    def half_of(chunk, half):
        return bias.at[chunk, half]

    def ring_copy(sign, k, half):
        i = 0 if sign > 0 else 1
        ref = half_of(lax.rem(z - sign * (k - 1) + 8, 8), half)
        return remote(ref, ref, ring_send.at[i, k - 1, half], ring_recv.at[i, k - 1, half], along_z(sign))

    def ring_arrived(sign, k, half):
        ref = half_of(lax.rem(z - sign * k + 8, 8), half)
        wait_bytes(ref, ring_recv.at[0 if sign > 0 else 1, k - 1, half])

    def goes(sign, k, half):
        return k < 4 or (k == 4 and half == (0 if sign > 0 else 1))

    def take(sign, k, half):
        if goes(sign, k, half):
            ring_arrived(sign, k, half)
        if goes(sign, k + 1, half):
            ring_copy(sign, k + 1, half).start()

    def qkv_copy(d, p):
        to = lax.rem(chip + d, 8)
        return remote(qkv.at[to, p], came.at[p, core, chip], qkv_send.at[p, d], qkv_recv.at[p], at(to, core))

    x_gain, x_shift = column(gain_ref[...], 2 * RES), column(shift_ref[...], 2 * RES)
    x_copy.wait()
    for c in w_copies:
        c.wait()
    wt = [w_v[i].astype(F32).T.astype(BF) for i in range(4)]

    def project(p):
        turned = jnp.concatenate([x_v[2 * p].T, x_v[2 * p + 1].T], 1).astype(F32)
        normed = (normalize(turned, x_gain) + x_shift).astype(BF)
        normed_v[p] = normed
        for j in range(3):
            y = jnp.dot(wt[j], normed, preferred_element_type=F32)
            if j == 2:
                y = y * HD ** (-0.5)
            y = y.astype(BF)
            for h in range(H):
                for s in range(2):
                    qkv[h, p, j, s * HD : (s + 1) * HD, :] = y[h * HD : (h + 1) * HD, s * RES : (s + 1) * RES]

    def send_pair(p):
        pltpu.make_async_copy(qkv.at[chip, p], came.at[p, core, chip], qkv_recv.at[p]).start()
        for d in range(1, 8):
            qkv_copy(d, p).start()

    for p in range(PAIRS):
        project(p)
        for half in range(2):
            if p == START_AT[half]:
                wait_bytes(half_of(z, half), bias_recv.at[half])
                for sign in (1, -1):
                    ring_copy(sign, 1, half).start()
        if p not in SEND_AT.values():
            send_pair(p)

    gate_shift = column(gs_ref[...], 2 * RES)
    for p in range(PAIRS):
        g = jax.nn.sigmoid(jnp.dot(wt[3], normed_v[p], preferred_element_type=F32) + gate_shift)
        for h in range(H):
            for s in range(2):
                gate[h, (2 * p + s) * HD : (2 * p + s + 1) * HD, :] = g[
                    h * HD : (h + 1) * HD, s * RES : (s + 1) * RES
                ]

    last = lax.rem(z + 4, 8)

    def gate_copy(d):
        to = lax.rem(chip + d, 8)
        return remote(gate.at[to], gate_in, gate_send.at[d], gate_recv, at(to, core))

    def send_gate():
        pltpu.make_async_copy(gate.at[chip], gate_in, gate_recv).start()
        for d in range(1, 8):
            gate_copy(d).start()

    def core_copy(p):
        ref = came.at[p, core, :, pl.ds(0, 2)]
        return remote(ref, ref, core_send.at[p], core_recv.at[p], sibling)

    def turn_keys(p, half):
        for b in range(8):
            rows = pl.ds(aligned(half * 1024 + b * RES, RES), RES)
            kn[p, rows, :] = came[p, half, b, 0].astype(F32).T.astype(BF)

    def pair_arrived(p):
        wait_bytes(came.at[p, core], qkv_recv.at[p])
        core_copy(p).start()
        turn_keys(p, core)
        wait_bytes(came.at[p, 1 - core, :, pl.ds(0, 2)], core_recv.at[p])
        turn_keys(p, 1 - core)

    def chunk_of(k):
        far = jnp.where(lax.rem(k, 2) == 1, -((k + 1) // 2), k // 2)
        return lax.rem(z + far + 8, 8)

    def place(v):
        w = v - 15
        k = jnp.where(v < 9, v // 3, jnp.where(v < 15, lax.rem(v, 3), 3 + w // PAIRS))
        p = jnp.where(v < 9, lax.rem(v, 3), jnp.where(v < 15, v // 3, lax.rem(v, PAIRS)))
        return k, p

    def before(v):
        k, p = place(v)

        for unit, hop, half in RING_AT:

            @pl.when(v == unit)
            def _(hop=hop, half=half):
                for sign in (1, -1):
                    take(sign, hop, half)
                    if hop == 4:
                        take(sign, hop, 1)

        @pl.when(jnp.logical_and(v == GATE_AT, chip == last))
        def _():
            send_gate()

        @pl.when(jnp.logical_and(k == 0, v < 15))
        def _():
            pair_arrived(p)

        for unit, pair in SEND_AT.items():

            @pl.when(v == unit)
            def _(pair=pair):
                send_pair(pair)

    def after(k, p):
        to = chunk_of(k)
        rows = pl.ds(aligned(p * PW, PW), PW)

        def send(src, dst, send_sem, recv_sem):
            @pl.when(to != chip)
            def _():
                remote(src, dst, send_sem, recv_sem, at(to, core)).start()

            @pl.when(to == chip)
            def _():
                pltpu.make_async_copy(src, dst, recv_sem).start()

        @pl.when(k < 7)
        def _():
            send(o.at[k, rows, :], back.at[chip, rows, :], back_send, back_recv)

        @pl.when(k == 7)
        def _():
            send(o_last.at[rows, :], gated_v.at[chip, rows, :], last_send, last_recv)

    def rhs_of(chunk, p):
        q = came[p, core, chunk, 2]
        none = jnp.zeros((HD, RES), BF)
        return jnp.concatenate([jnp.concatenate([q[:HD], none], 1), jnp.concatenate([none, q[HD:]], 1)], 0)

    def score_tile(t, rhs, p, chunk, s, top):
        rows = pl.ds(t * TILE, TILE)
        b = jnp.concatenate(
            [
                bias[chunk, half, pl.ds((t * TILE // RES + i) * HALF, HALF), :]
                for i in range(TILE // RES)
                for half in range(2)
            ],
            0,
        ).astype(F32)
        scores = jnp.dot(kn[p, rows, :], rhs, preferred_element_type=F32) + jnp.concatenate([b, b], 1)
        s[rows, :] = scores
        return jnp.maximum(top, jnp.max(scores.reshape(TILE // 8, 8, 2 * RES), axis=0))

    def value_tile(t, p, s, top, total, acc):
        e = jnp.exp(s[pl.ds(t * TILE, TILE), :] - top)
        total = total + jnp.sum(e.reshape(TILE // 8, 8, 2 * RES), axis=0)
        v = [came[p, (t * TILE) // 1024, (t * TILE) % 1024 // RES + i, 1] for i in range(TILE // RES)]
        return total, acc + jnp.dot(jnp.concatenate(v, 1), e.astype(BF), preferred_element_type=F32)

    lowest = jnp.full((8, 2 * RES), -jnp.inf, F32)
    steps = KEYS // TILE
    units = 8 * PAIRS

    def first(s):
        zero = jnp.int32(0)
        before(zero)
        rhs = rhs_of(z, zero)
        top = lowest
        for t in range(steps):
            top = score_tile(t, rhs, zero, z, s, top)
        return top

    def both(u, top, s_now, s_next):
        before(u + 1)
        k, p = place(u)
        kv, pv = place(jnp.minimum(u + 1, units - 1))
        chunk = chunk_of(kv)
        top = jnp.max(top, axis=0, keepdims=True)
        rhs = rhs_of(chunk, pv)
        total = jnp.zeros((8, 2 * RES), F32)
        acc = jnp.zeros((PW, 2 * RES), F32)
        top_next = lowest
        for t in range(steps):
            top_next = score_tile(t, rhs, pv, chunk, s_next, top_next)
            total, acc = value_tile(t, p, s_now, top, total, acc)
        result = acc / jnp.sum(total, axis=0, keepdims=True)
        halves = (result[:HD, :RES], result[HD:, RES:])

        @pl.when(k < 7)
        def _():
            for i, half in enumerate(halves):
                o[k, pl.ds(aligned(p * PW + i * HD, HD), HD), :] = half

        @pl.when(k == 7)
        def _():
            @pl.when(p == 0)
            def _():
                wait_bytes(gate_in, gate_recv)

            for i, half in enumerate(halves):
                rows = pl.ds(aligned(p * PW + i * HD, HD), HD)
                o_last[rows, :] = (gate_in[rows, :] * half).astype(BF)

        after(k, p)
        return top_next

    def body(i, top):
        top = both(2 * i, top, sa, sb)
        return both(2 * i + 1, top, sb, sa)

    lax.fori_loop(0, units // 2, body, first(sa))

    @pl.when(chip != last)
    def _():
        wait_bytes(back, back_recv)
        for h in range(H):
            gated_v[h] = (gate[h] * back[h]).astype(BF)

    @pl.when(chip == last)
    def _():
        wait_bytes(gated_v, last_recv)

    wo = w_v[4]
    for s in range(SEQS):
        gated = jnp.concatenate([gated_v[h, s * HD : (s + 1) * HD, :] for h in range(H)], 0)
        out[s] = jnp.dot(gated.T, wo, preferred_element_type=F32).astype(BF)

    @pl.when(chip != last)
    def _():
        wait_bytes(o.at[pl.ds(0, 6)], back_send)
        wait_bytes(o_last, last_send)

    @pl.when(chip == last)
    def _():
        wait_bytes(o.at[pl.ds(0, 7)], back_send)
        for d in range(1, 8):
            gate_copy(d).wait_send()
    for half in range(2):
        for d in range(8):
            tile_copy(half, d, 1).wait_send()
            if d:
                tile_copy(half, d, 0).wait_send()

        @pl.when(jnp.logical_not(owner))
        def _(half=half):
            tile_copy(half, 0, 0).wait_send()

    for p in range(PAIRS):
        for d in range(1, 8):
            qkv_copy(d, p).wait_send()
        core_copy(p).wait_send()
    for sign in (1, -1):
        for half in range(2):
            for k in range(1, 5):
                if goes(sign, k, half):
                    ring_copy(sign, k, half).wait_send()


def local(x, pair, x_gain, x_shift, pair_gain, wq, wk, wv, wg, gate_shift, w_bias, w_out):
    dma = pltpu.SemaphoreType.DMA
    return pl.pallas_call(
        kernel,
        name="attention",
        out_shape=jax.ShapeDtypeStruct((SEQS, RES, CH), BF),
        in_specs=[HBM, HBM, VMEM, VMEM, VMEM, HBM, HBM, HBM, HBM, VMEM, VMEM, HBM],
        out_specs=VMEM,
        scratch_shapes=[
            pltpu.VMEM((RES, RES, CP), BF),
            pltpu.VMEM((SEQS, RES, CH), BF),
            pltpu.VMEM((5, CH, CH), BF),
            pltpu.VMEM((HALF * H, RES), F32),
            pltpu.VMEM((2, H, HALF, RES), BF),
            pltpu.VMEM((PAIRS, CH, 2 * RES), BF),
            pltpu.VMEM((H, PAIRS, 3, PW, RES), BF),
            pltpu.VMEM((H, ROWS, RES), F32),
            pltpu.VMEM((ROWS, RES), F32),
            pltpu.VMEM((PAIRS, 2, 8, 3, PW, RES), BF),
            pltpu.VMEM((8, 2, KEYS // 2, RES), BF),
            pltpu.VMEM((PAIRS, KEYS, PW), BF),
            pltpu.VMEM((KEYS, 2 * RES), F32),
            pltpu.VMEM((KEYS, 2 * RES), F32),
            pltpu.VMEM((7, ROWS, RES), F32),
            pltpu.VMEM((ROWS, RES), BF),
            pltpu.VMEM((8, ROWS, RES), F32),
            pltpu.VMEM((8, ROWS, RES), BF),
            dma((2, RES // STEP)),
            dma,
            dma((5,)),
            dma((2, 2, 8)),
            dma((PAIRS, 8)),
            dma((8,)),
            dma((PAIRS,)),
            dma((2, 4, 2)),
            dma,
            dma,
            dma((2,)),
            dma((PAIRS,)),
            dma,
            dma((PAIRS,)),
            dma((2, 4, 2)),
            dma,
            dma,
        ],
        compiler_params=pltpu.CompilerParams(
            collective_id=0, has_side_effects=True, vmem_limit_bytes=LIMIT
        ),
    )(
        x, pair, x_gain.reshape(1, CH), x_shift.reshape(1, CH), pair_gain.reshape(1, CP),
        wq, wk, wv, wg, gate_shift.reshape(1, CH), w_bias.T, w_out,
    )


def solution(mesh):
    split = P("seq", "res", None)
    in_specs = (split, split) + (P(),) * 10
    return jax.shard_map(local, mesh=mesh, in_specs=in_specs, out_specs=split, check_vma=False)
```

```python
import jax
import jax.numpy as jnp
from jax import lax
from jax.experimental import pallas as pl
from jax.experimental.pallas import tpu as pltpu
from jax.sharding import PartitionSpec as P

F32, BF = jnp.float32, jnp.bfloat16
MESH = pl.DeviceIdType.MESH
VMEM = pl.BlockSpec(memory_space=pltpu.VMEM)
HBM = pl.BlockSpec(memory_space=pl.ANY)

H, HD = 8, 32
SEQS, RES, CH, CP = 10, 128, 256, 128
KEYS = 2048
ROWS = SEQS * HD
PAIRS = SEQS // 2
PW = 2 * HD
TILE = 256
HALF = RES // 2
STEP = 16
LIMIT = 60 * 2**20
RING_AT = ((1, 1, 0), (2, 1, 1), (9, 2, 0), (12, 2, 1), (20, 3, 0), (25, 3, 1), (35, 4, 0))
SEND_AT = {}
GATE_AT = 9
START_AT = (0, 1)


def aligned(value, n):
    return pl.multiple_of(value, n)


def column(row, n):
    return jnp.broadcast_to(row, (n, row.shape[1])).T


def normalize(values, gain):
    mean = jnp.mean(values, axis=0, keepdims=True)
    centered = values - mean
    var = jnp.mean(centered * centered, axis=0, keepdims=True)
    return centered * lax.rsqrt(var + 1e-05) * gain


def kernel(
    x_hbm, pair_hbm, gain_ref, shift_ref, pair_gain_ref, wq_hbm, wk_hbm, wv_hbm, wg_hbm, gs_ref, wb_ref, wo_hbm,
    out,
    pair_v, x_v, w_v, logits, tiles, normed_v, qkv, gate, gate_in, came, bias, kn, sa, sb, o, o_last, back, gated_v,
    pair_in, x_in, w_in,
    tile_send, qkv_send, gate_send, core_send, ring_send, back_send, last_send,
    bias_recv, qkv_recv, gate_recv, core_recv, ring_recv, back_recv, last_recv,
):
    seq, res = lax.axis_index("seq"), lax.axis_index("res")
    z, low = seq // 2, lax.rem(seq, 2)
    chip, core = res // 2, lax.rem(res, 2)
    owner = core == low

    def pair_copy(half, i):
        rows, keys = pl.ds(i * STEP, STEP), pl.ds(half * HALF, HALF)
        return pltpu.make_async_copy(pair_hbm.at[rows, keys], pair_v.at[rows, keys], pair_in.at[half, i])

    for half in range(2):
        for i in range(RES // STEP):
            pair_copy(half, i).start()
    x_copy = pltpu.make_async_copy(x_hbm, x_v, x_in)
    x_copy.start()
    w_copies = [
        pltpu.make_async_copy(w, w_v.at[i], w_in.at[i])
        for i, w in enumerate((wk_hbm, wv_hbm, wq_hbm, wg_hbm, wo_hbm))
    ]
    for c in w_copies:
        c.start()

    def at(other_chip, other_core):
        return (seq, other_chip * 2 + other_core)

    def along_z(d):
        return (lax.rem(z + d + 8, 8) * 2 + low, res)

    sibling = at(chip, 1 - core)

    def remote(src, dst, send, recv, device):
        return pltpu.make_async_remote_copy(
            src_ref=src, dst_ref=dst, send_sem=send, recv_sem=recv, device_id=device, device_id_type=MESH
        )

    def wait_bytes(ref, sem):
        pltpu.make_async_copy(ref, ref, sem).wait()

    barrier = pltpu.get_barrier_semaphore()
    for other in range(2):
        for d in range(other ^ 1, 16):
            peer = (z * 2 + lax.rem(low + other, 2), lax.rem(res + d, 16))
            pl.semaphore_signal(barrier, inc=1, device_id=peer, device_id_type=MESH)
    for sign in (1, -1):
        pl.semaphore_signal(barrier, inc=1, device_id=along_z(sign), device_id_type=MESH)

    pair_gain = column(pair_gain_ref[...], RES)
    pair_gain = jnp.concatenate([pair_gain, pair_gain], 1)
    wb = wb_ref[...]

    mine = pl.ds(aligned((core * 8 + chip) * HALF, HALF), HALF)

    def logits_of(half):
        keys = slice(half * HALF, (half + 1) * HALF)

        def pair_step(i, carry):
            pair_copy(half, i).wait()
            pair_copy(half, i + RES // STEP // 2).wait()
            for j in range(STEP // 2):
                row = i * STEP + 2 * j
                blocks = [
                    jnp.concatenate([pair_v[row + k, keys, :], pair_v[row + k + HALF, keys, :]], 0).T
                    for k in range(2)
                ]
                turned = jnp.concatenate(blocks, 1).astype(F32)
                y = jnp.dot(wb, normalize(turned, pair_gain).astype(BF), preferred_element_type=F32)
                at_row = aligned(row * H, 2 * H)
                logits[pl.ds(at_row, H), :] = y[:, :RES]
                logits[pl.ds(at_row + H, H), :] = y[:, RES:]
            return carry

        lax.fori_loop(0, RES // STEP // 2, pair_step, 0)
        for h in range(H):
            t = logits[pl.ds(h, HALF, stride=H), :].T
            tiles[half, h] = jnp.concatenate([t[:HALF], t[HALF:]], 1).astype(BF)

    def tile_copy(half, d, other):
        to = lax.rem(chip + d, 8)
        device = (z * 2 + lax.rem(low + other, 2), to * 2 + low)
        return remote(
            tiles.at[half, to], bias.at[z, half, mine, :], tile_send.at[half, other, d], bias_recv.at[half], device
        )

    def send_tiles(half):
        @pl.when(owner)
        def _():
            pltpu.make_async_copy(tiles.at[half, chip], bias.at[z, half, mine, :], bias_recv.at[half]).start()

        @pl.when(jnp.logical_not(owner))
        def _():
            tile_copy(half, 0, 0).start()

        tile_copy(half, 0, 1).start()
        for d in range(1, 8):
            for other in range(2):
                tile_copy(half, d, other).start()

    logits_of(0)
    pl.semaphore_wait(barrier, 33)
    send_tiles(0)
    logits_of(1)
    send_tiles(1)

    def half_of(chunk, half):
        return bias.at[chunk, half]

    def ring_copy(sign, k, half):
        i = 0 if sign > 0 else 1
        ref = half_of(lax.rem(z - sign * (k - 1) + 8, 8), half)
        return remote(ref, ref, ring_send.at[i, k - 1, half], ring_recv.at[i, k - 1, half], along_z(sign))

    def ring_arrived(sign, k, half):
        ref = half_of(lax.rem(z - sign * k + 8, 8), half)
        wait_bytes(ref, ring_recv.at[0 if sign > 0 else 1, k - 1, half])

    def goes(sign, k, half):
        return k < 4 or (k == 4 and half == (0 if sign > 0 else 1))

    def take(sign, k, half):
        if goes(sign, k, half):
            ring_arrived(sign, k, half)
        if goes(sign, k + 1, half):
            ring_copy(sign, k + 1, half).start()

    def qkv_copy(d, p):
        to = lax.rem(chip + d, 8)
        return remote(qkv.at[to, p], came.at[p, core, chip], qkv_send.at[p, d], qkv_recv.at[p], at(to, core))

    x_gain, x_shift = column(gain_ref[...], 2 * RES), column(shift_ref[...], 2 * RES)
    x_copy.wait()
    for c in w_copies:
        c.wait()
    wt = [w_v[i].astype(F32).T.astype(BF) for i in range(4)]

    def project(p):
        turned = jnp.concatenate([x_v[2 * p].T, x_v[2 * p + 1].T], 1).astype(F32)
        normed = (normalize(turned, x_gain) + x_shift).astype(BF)
        normed_v[p] = normed
        for j in range(3):
            y = jnp.dot(wt[j], normed, preferred_element_type=F32)
            if j == 2:
                y = y * HD ** (-0.5)
            y = y.astype(BF)
            for h in range(H):
                for s in range(2):
                    qkv[h, p, j, s * HD : (s + 1) * HD, :] = y[h * HD : (h + 1) * HD, s * RES : (s + 1) * RES]

    def send_pair(p):
        pltpu.make_async_copy(qkv.at[chip, p], came.at[p, core, chip], qkv_recv.at[p]).start()
        for d in range(1, 8):
            qkv_copy(d, p).start()

    for p in range(PAIRS):
        project(p)
        for half in range(2):
            if p == START_AT[half]:
                wait_bytes(half_of(z, half), bias_recv.at[half])
                for sign in (1, -1):
                    ring_copy(sign, 1, half).start()
        if p not in SEND_AT.values():
            send_pair(p)

    gate_shift = column(gs_ref[...], 2 * RES)
    for p in range(PAIRS):
        g = jax.nn.sigmoid(jnp.dot(wt[3], normed_v[p], preferred_element_type=F32) + gate_shift)
        for h in range(H):
            for s in range(2):
                gate[h, (2 * p + s) * HD : (2 * p + s + 1) * HD, :] = g[
                    h * HD : (h + 1) * HD, s * RES : (s + 1) * RES
                ]

    last = lax.rem(z + 4, 8)

    def gate_copy(d):
        to = lax.rem(chip + d, 8)
        return remote(gate.at[to], gate_in, gate_send.at[d], gate_recv, at(to, core))

    def send_gate():
        pltpu.make_async_copy(gate.at[chip], gate_in, gate_recv).start()
        for d in range(1, 8):
            gate_copy(d).start()

    def core_copy(p):
        ref = came.at[p, core, :, pl.ds(0, 2)]
        return remote(ref, ref, core_send.at[p], core_recv.at[p], sibling)

    def turn_keys(p, half):
        for b in range(8):
            rows = pl.ds(aligned(half * 1024 + b * RES, RES), RES)
            kn[p, rows, :] = came[p, half, b, 0].astype(F32).T.astype(BF)

    def pair_arrived(p):
        wait_bytes(came.at[p, core], qkv_recv.at[p])
        core_copy(p).start()
        turn_keys(p, core)
        wait_bytes(came.at[p, 1 - core, :, pl.ds(0, 2)], core_recv.at[p])
        turn_keys(p, 1 - core)

    def chunk_of(k):
        far = jnp.where(lax.rem(k, 2) == 1, -((k + 1) // 2), k // 2)
        return lax.rem(z + far + 8, 8)

    def place(v):
        w = v - 15
        k = jnp.where(v < 9, v // 3, jnp.where(v < 15, lax.rem(v, 3), 3 + w // PAIRS))
        p = jnp.where(v < 9, lax.rem(v, 3), jnp.where(v < 15, v // 3, lax.rem(v, PAIRS)))
        return k, p

    def before(v):
        @pl.when(jnp.logical_or(v < 15, lax.rem(v, PAIRS) == 0))
        def _():
            before_some(v)

    def before_some(v):
        k, p = place(v)

        for unit, hop, half in RING_AT:

            @pl.when(v == unit)
            def _(hop=hop, half=half):
                for sign in (1, -1):
                    take(sign, hop, half)
                    if hop == 4:
                        take(sign, hop, 1)

        @pl.when(jnp.logical_and(v == GATE_AT, chip == last))
        def _():
            send_gate()

        @pl.when(jnp.logical_and(k == 0, v < 15))
        def _():
            pair_arrived(p)

        for unit, pair in SEND_AT.items():

            @pl.when(v == unit)
            def _(pair=pair):
                send_pair(pair)

    def after(k, p, halves):
        to = chunk_of(k)
        rows = pl.ds(aligned(p * PW, PW), PW)

        def send(src, dst, send_sem, recv_sem):
            @pl.when(to != chip)
            def _():
                remote(src, dst, send_sem, recv_sem, at(to, core)).start()

            @pl.when(to == chip)
            def _():
                pltpu.make_async_copy(src, dst, recv_sem).start()

        @pl.when(k < 7)
        def _():
            for i, half in enumerate(halves):
                o[k, pl.ds(aligned(p * PW + i * HD, HD), HD), :] = half
            send(o.at[k, rows, :], back.at[chip, rows, :], back_send, back_recv)

        @pl.when(k == 7)
        def _():
            @pl.when(p == 0)
            def _():
                wait_bytes(gate_in, gate_recv)

            for i, half in enumerate(halves):
                part = pl.ds(aligned(p * PW + i * HD, HD), HD)
                o_last[part, :] = (gate_in[part, :] * half).astype(BF)
            send(o_last.at[rows, :], gated_v.at[chip, rows, :], last_send, last_recv)

    def rhs_of(chunk, p):
        q = came[p, core, chunk, 2]
        none = jnp.zeros((HD, RES), BF)
        return jnp.concatenate([jnp.concatenate([q[:HD], none], 1), jnp.concatenate([none, q[HD:]], 1)], 0)

    def score_tile(t, rhs, p, chunk, s, top):
        rows = pl.ds(t * TILE, TILE)
        b = jnp.concatenate(
            [
                bias[chunk, half, pl.ds((t * TILE // RES + i) * HALF, HALF), :]
                for i in range(TILE // RES)
                for half in range(2)
            ],
            0,
        ).astype(F32)
        scores = jnp.dot(kn[p, rows, :], rhs, preferred_element_type=F32) + jnp.concatenate([b, b], 1)
        s[rows, :] = scores
        return jnp.maximum(top, jnp.max(scores.reshape(TILE // 8, 8, 2 * RES), axis=0))

    def value_tile(t, p, s, top, total, acc):
        e = jnp.exp(s[pl.ds(t * TILE, TILE), :] - top)
        total = total + jnp.sum(e.reshape(TILE // 8, 8, 2 * RES), axis=0)
        v = [came[p, (t * TILE) // 1024, (t * TILE) % 1024 // RES + i, 1] for i in range(TILE // RES)]
        return total, acc + jnp.dot(jnp.concatenate(v, 1), e.astype(BF), preferred_element_type=F32)

    lowest = jnp.full((8, 2 * RES), -jnp.inf, F32)
    steps = KEYS // TILE
    units = 8 * PAIRS

    def first(s):
        zero = jnp.int32(0)
        before(zero)
        rhs = rhs_of(z, zero)
        top = lowest
        for t in range(steps):
            top = score_tile(t, rhs, zero, z, s, top)
        return top

    def both(u, top, s_now, s_next):
        before(u + 1)
        k, p = place(u)
        kv, pv = place(jnp.minimum(u + 1, units - 1))
        chunk = chunk_of(kv)
        top = jnp.max(top, axis=0, keepdims=True)
        rhs = rhs_of(chunk, pv)
        total = jnp.zeros((8, 2 * RES), F32)
        acc = jnp.zeros((PW, 2 * RES), F32)
        top_next = lowest
        for t in range(steps):
            top_next = score_tile(t, rhs, pv, chunk, s_next, top_next)
            total, acc = value_tile(t, p, s_now, top, total, acc)
        result = acc / jnp.sum(total, axis=0, keepdims=True)
        after(k, p, (result[:HD, :RES], result[HD:, RES:]))
        return top_next

    def body(i, top):
        top = both(2 * i, top, sa, sb)
        return both(2 * i + 1, top, sb, sa)

    lax.fori_loop(0, units // 2, body, first(sa))

    @pl.when(chip != last)
    def _():
        wait_bytes(back, back_recv)
        for h in range(H):
            gated_v[h] = (gate[h] * back[h]).astype(BF)

    @pl.when(chip == last)
    def _():
        wait_bytes(gated_v, last_recv)

    wo = w_v[4]
    for s in range(SEQS):
        gated = jnp.concatenate([gated_v[h, s * HD : (s + 1) * HD, :] for h in range(H)], 0)
        out[s] = jnp.dot(gated.T, wo, preferred_element_type=F32).astype(BF)

    @pl.when(chip != last)
    def _():
        wait_bytes(o.at[pl.ds(0, 6)], back_send)
        wait_bytes(o_last, last_send)

    @pl.when(chip == last)
    def _():
        wait_bytes(o.at[pl.ds(0, 7)], back_send)
        for d in range(1, 8):
            gate_copy(d).wait_send()
    for half in range(2):
        for d in range(8):
            tile_copy(half, d, 1).wait_send()
            if d:
                tile_copy(half, d, 0).wait_send()

        @pl.when(jnp.logical_not(owner))
        def _(half=half):
            tile_copy(half, 0, 0).wait_send()

    for p in range(PAIRS):
        for d in range(1, 8):
            qkv_copy(d, p).wait_send()
        core_copy(p).wait_send()
    for sign in (1, -1):
        for half in range(2):
            for k in range(1, 5):
                if goes(sign, k, half):
                    ring_copy(sign, k, half).wait_send()


def local(x, pair, x_gain, x_shift, pair_gain, wq, wk, wv, wg, gate_shift, w_bias, w_out):
    dma = pltpu.SemaphoreType.DMA
    return pl.pallas_call(
        kernel,
        name="attention",
        out_shape=jax.ShapeDtypeStruct((SEQS, RES, CH), BF),
        in_specs=[HBM, HBM, VMEM, VMEM, VMEM, HBM, HBM, HBM, HBM, VMEM, VMEM, HBM],
        out_specs=VMEM,
        scratch_shapes=[
            pltpu.VMEM((RES, RES, CP), BF),
            pltpu.VMEM((SEQS, RES, CH), BF),
            pltpu.VMEM((5, CH, CH), BF),
            pltpu.VMEM((HALF * H, RES), F32),
            pltpu.VMEM((2, H, HALF, RES), BF),
            pltpu.VMEM((PAIRS, CH, 2 * RES), BF),
            pltpu.VMEM((H, PAIRS, 3, PW, RES), BF),
            pltpu.VMEM((H, ROWS, RES), F32),
            pltpu.VMEM((ROWS, RES), F32),
            pltpu.VMEM((PAIRS, 2, 8, 3, PW, RES), BF),
            pltpu.VMEM((8, 2, KEYS // 2, RES), BF),
            pltpu.VMEM((PAIRS, KEYS, PW), BF),
            pltpu.VMEM((KEYS, 2 * RES), F32),
            pltpu.VMEM((KEYS, 2 * RES), F32),
            pltpu.VMEM((7, ROWS, RES), F32),
            pltpu.VMEM((ROWS, RES), BF),
            pltpu.VMEM((8, ROWS, RES), F32),
            pltpu.VMEM((8, ROWS, RES), BF),
            dma((2, RES // STEP)),
            dma,
            dma((5,)),
            dma((2, 2, 8)),
            dma((PAIRS, 8)),
            dma((8,)),
            dma((PAIRS,)),
            dma((2, 4, 2)),
            dma,
            dma,
            dma((2,)),
            dma((PAIRS,)),
            dma,
            dma((PAIRS,)),
            dma((2, 4, 2)),
            dma,
            dma,
        ],
        compiler_params=pltpu.CompilerParams(
            collective_id=0, has_side_effects=True, vmem_limit_bytes=LIMIT
        ),
    )(
        x, pair, x_gain.reshape(1, CH), x_shift.reshape(1, CH), pair_gain.reshape(1, CP),
        wq, wk, wv, wg, gate_shift.reshape(1, CH), w_bias.T, w_out,
    )


def solution(mesh):
    split = P("seq", "res", None)
    in_specs = (split, split) + (P(),) * 10
    return jax.shard_map(local, mesh=mesh, in_specs=in_specs, out_specs=split, check_vma=False)
```

```python
import jax
import jax.numpy as jnp
from jax import lax
from jax.experimental import pallas as pl
from jax.experimental.pallas import tpu as pltpu
from jax.sharding import PartitionSpec as P

F32, BF = jnp.float32, jnp.bfloat16
MESH = pl.DeviceIdType.MESH
VMEM = pl.BlockSpec(memory_space=pltpu.VMEM)
HBM = pl.BlockSpec(memory_space=pl.ANY)

H, HD = 8, 32
SEQS, RES, CH, CP = 10, 128, 256, 128
KEYS = 2048
ROWS = SEQS * HD
PAIRS = SEQS // 2
PW = 2 * HD
TILE = 256
HALF = RES // 2
STEP = 16
LIMIT = 60 * 2**20
RING_AT = ((1, 1, 0), (2, 1, 1), (9, 2, 0), (12, 2, 1), (20, 3, 0), (25, 3, 1), (35, 4, 0))
SEND_AT = {}
GATE_AT = 9
START_AT = (0, 1)


def aligned(value, n):
    return pl.multiple_of(value, n)


def column(row, n):
    return jnp.broadcast_to(row, (n, row.shape[1])).T


def normalize(values, gain):
    mean = jnp.mean(values, axis=0, keepdims=True)
    centered = values - mean
    var = jnp.mean(centered * centered, axis=0, keepdims=True)
    return centered * lax.rsqrt(var + 1e-05) * gain


def kernel(
    x_hbm, pair_hbm, gain_ref, shift_ref, pair_gain_ref, wq_hbm, wk_hbm, wv_hbm, wg_hbm, gs_ref, wb_ref, wo_hbm,
    out,
    pair_v, x_v, w_v, logits, tiles, normed_v, qkv, gate, gate_in, came, bias, kn, sa, sb, o, o_last, back, gated_v,
    pair_in, x_in, w_in,
    tile_send, qkv_send, gate_send, core_send, ring_send, back_send, last_send,
    bias_recv, qkv_recv, gate_recv, core_recv, ring_recv, back_recv, last_recv,
):
    seq, res = lax.axis_index("seq"), lax.axis_index("res")
    z, low = seq // 2, lax.rem(seq, 2)
    chip, core = res // 2, lax.rem(res, 2)
    owner = core == low

    def pair_copy(half, i):
        rows, keys = pl.ds(i * STEP, STEP), pl.ds(half * HALF, HALF)
        return pltpu.make_async_copy(pair_hbm.at[rows, keys], pair_v.at[rows, keys], pair_in.at[half, i])

    for half in range(2):
        for i in range(RES // STEP):
            pair_copy(half, i).start()
    x_copy = pltpu.make_async_copy(x_hbm, x_v, x_in)
    x_copy.start()
    w_copies = [
        pltpu.make_async_copy(w, w_v.at[i], w_in.at[i])
        for i, w in enumerate((wk_hbm, wv_hbm, wq_hbm, wg_hbm, wo_hbm))
    ]
    for c in w_copies:
        c.start()

    def at(other_chip, other_core):
        return (seq, other_chip * 2 + other_core)

    def along_z(d):
        return (lax.rem(z + d + 8, 8) * 2 + low, res)

    sibling = at(chip, 1 - core)

    def remote(src, dst, send, recv, device):
        return pltpu.make_async_remote_copy(
            src_ref=src, dst_ref=dst, send_sem=send, recv_sem=recv, device_id=device, device_id_type=MESH
        )

    def wait_bytes(ref, sem):
        pltpu.make_async_copy(ref, ref, sem).wait()

    barrier = pltpu.get_barrier_semaphore()
    for other in range(2):
        for d in range(other ^ 1, 16):
            peer = (z * 2 + lax.rem(low + other, 2), lax.rem(res + d, 16))
            pl.semaphore_signal(barrier, inc=1, device_id=peer, device_id_type=MESH)
    for sign in (1, -1):
        pl.semaphore_signal(barrier, inc=1, device_id=along_z(sign), device_id_type=MESH)

    pair_gain = column(pair_gain_ref[...], RES)
    pair_gain = jnp.concatenate([pair_gain, pair_gain], 1)
    wb = wb_ref[...]

    mine = pl.ds(aligned((core * 8 + chip) * HALF, HALF), HALF)

    def logits_of(half):
        keys = slice(half * HALF, (half + 1) * HALF)

        def pair_step(i, carry):
            pair_copy(half, i).wait()
            pair_copy(half, i + RES // STEP // 2).wait()
            for j in range(STEP // 2):
                row = i * STEP + 2 * j
                blocks = [
                    jnp.concatenate([pair_v[row + k, keys, :], pair_v[row + k + HALF, keys, :]], 0).T
                    for k in range(2)
                ]
                turned = jnp.concatenate(blocks, 1).astype(F32)
                y = jnp.dot(wb, normalize(turned, pair_gain).astype(BF), preferred_element_type=F32)
                at_row = aligned(row * H, 2 * H)
                logits[pl.ds(at_row, H), :] = y[:, :RES]
                logits[pl.ds(at_row + H, H), :] = y[:, RES:]
            return carry

        lax.fori_loop(0, RES // STEP // 2, pair_step, 0)
        for h in range(H):
            t = logits[pl.ds(h, HALF, stride=H), :].T
            tiles[half, h] = jnp.concatenate([t[:HALF], t[HALF:]], 1).astype(BF)

    def tile_copy(half, d, other):
        to = lax.rem(chip + d, 8)
        device = (z * 2 + lax.rem(low + other, 2), to * 2 + low)
        return remote(
            tiles.at[half, to], bias.at[z, half, mine, :], tile_send.at[half, other, d], bias_recv.at[half], device
        )

    def send_tiles(half):
        @pl.when(owner)
        def _():
            pltpu.make_async_copy(tiles.at[half, chip], bias.at[z, half, mine, :], bias_recv.at[half]).start()

        @pl.when(jnp.logical_not(owner))
        def _():
            tile_copy(half, 0, 0).start()

        tile_copy(half, 0, 1).start()
        for d in range(1, 8):
            for other in range(2):
                tile_copy(half, d, other).start()

    logits_of(0)
    pl.semaphore_wait(barrier, 33)
    send_tiles(0)
    logits_of(1)
    send_tiles(1)

    def half_of(chunk, half):
        return bias.at[chunk, half]

    def ring_copy(sign, k, half):
        i = 0 if sign > 0 else 1
        ref = half_of(lax.rem(z - sign * (k - 1) + 8, 8), half)
        return remote(ref, ref, ring_send.at[i, k - 1, half], ring_recv.at[i, k - 1, half], along_z(sign))

    def ring_arrived(sign, k, half):
        ref = half_of(lax.rem(z - sign * k + 8, 8), half)
        wait_bytes(ref, ring_recv.at[0 if sign > 0 else 1, k - 1, half])

    def goes(sign, k, half):
        return k < 4 or (k == 4 and half == (0 if sign > 0 else 1))

    def take(sign, k, half):
        if goes(sign, k, half):
            ring_arrived(sign, k, half)
        if goes(sign, k + 1, half):
            ring_copy(sign, k + 1, half).start()

    def qkv_copy(d, p):
        to = lax.rem(chip + d, 8)
        return remote(qkv.at[to, p], came.at[p, core, chip], qkv_send.at[p, d], qkv_recv.at[p], at(to, core))

    x_gain, x_shift = column(gain_ref[...], 2 * RES), column(shift_ref[...], 2 * RES)
    x_copy.wait()
    for c in w_copies:
        c.wait()
    wt = [w_v[i].astype(F32).T.astype(BF) for i in range(4)]

    def project(p):
        turned = jnp.concatenate([x_v[2 * p].T, x_v[2 * p + 1].T], 1).astype(F32)
        normed = (normalize(turned, x_gain) + x_shift).astype(BF)
        normed_v[p] = normed
        for j in range(3):
            y = jnp.dot(wt[j], normed, preferred_element_type=F32)
            if j == 2:
                y = y * HD ** (-0.5)
            y = y.astype(BF)
            for h in range(H):
                for s in range(2):
                    qkv[h, p, j, s * HD : (s + 1) * HD, :] = y[h * HD : (h + 1) * HD, s * RES : (s + 1) * RES]

    def send_pair(p):
        pltpu.make_async_copy(qkv.at[chip, p], came.at[p, core, chip], qkv_recv.at[p]).start()
        for d in range(1, 8):
            qkv_copy(d, p).start()

    for p in range(PAIRS):
        project(p)
        for half in range(2):
            if p == START_AT[half]:
                wait_bytes(half_of(z, half), bias_recv.at[half])
                for sign in (1, -1):
                    ring_copy(sign, 1, half).start()
        if p not in SEND_AT.values():
            send_pair(p)

    gate_shift = column(gs_ref[...], 2 * RES)
    for p in range(PAIRS):
        g = jax.nn.sigmoid(jnp.dot(wt[3], normed_v[p], preferred_element_type=F32) + gate_shift)
        for h in range(H):
            for s in range(2):
                gate[h, (2 * p + s) * HD : (2 * p + s + 1) * HD, :] = g[
                    h * HD : (h + 1) * HD, s * RES : (s + 1) * RES
                ]

    last = lax.rem(z + 4, 8)

    def gate_copy(d):
        to = lax.rem(chip + d, 8)
        return remote(gate.at[to], gate_in, gate_send.at[d], gate_recv, at(to, core))

    def send_gate():
        pltpu.make_async_copy(gate.at[chip], gate_in, gate_recv).start()
        for d in range(1, 8):
            gate_copy(d).start()

    def core_copy(p):
        ref = came.at[p, core, :, pl.ds(0, 2)]
        return remote(ref, ref, core_send.at[p], core_recv.at[p], sibling)

    def turn_keys(p, half):
        for b in range(8):
            rows = pl.ds(aligned(half * 1024 + b * RES, RES), RES)
            kn[p, rows, :] = came[p, half, b, 0].astype(F32).T.astype(BF)

    def pair_arrived(p):
        wait_bytes(came.at[p, core], qkv_recv.at[p])
        core_copy(p).start()
        turn_keys(p, core)
        wait_bytes(came.at[p, 1 - core, :, pl.ds(0, 2)], core_recv.at[p])
        turn_keys(p, 1 - core)

    side = 1 - 2 * lax.rem(chip, 2)

    def chunk_of(k):
        far = jnp.where(lax.rem(k, 2) == 1, -((k + 1) // 2), k // 2)
        return lax.rem(z + side * far + 8, 8)

    def place(v):
        w = v - 15
        k = jnp.where(v < 9, v // 3, jnp.where(v < 15, lax.rem(v, 3), 3 + w // PAIRS))
        p = jnp.where(v < 9, lax.rem(v, 3), jnp.where(v < 15, v // 3, lax.rem(v, PAIRS)))
        return k, p

    def before(v):
        @pl.when(jnp.logical_or(v < 15, lax.rem(v, PAIRS) == 0))
        def _():
            before_some(v)

    def before_some(v):
        k, p = place(v)

        for unit, hop, half in RING_AT:

            @pl.when(v == unit)
            def _(hop=hop, half=half):
                for sign in (1, -1):
                    take(sign, hop, half)
                    if hop == 4:
                        take(sign, hop, 1)

        @pl.when(jnp.logical_and(v == GATE_AT, chip == last))
        def _():
            send_gate()

        @pl.when(jnp.logical_and(k == 0, v < 15))
        def _():
            pair_arrived(p)

        for unit, pair in SEND_AT.items():

            @pl.when(v == unit)
            def _(pair=pair):
                send_pair(pair)

    def after(k, p, halves):
        to = chunk_of(k)
        rows = pl.ds(aligned(p * PW, PW), PW)

        def send(src, dst, send_sem, recv_sem):
            @pl.when(to != chip)
            def _():
                remote(src, dst, send_sem, recv_sem, at(to, core)).start()

            @pl.when(to == chip)
            def _():
                pltpu.make_async_copy(src, dst, recv_sem).start()

        @pl.when(k < 7)
        def _():
            for i, half in enumerate(halves):
                o[k, pl.ds(aligned(p * PW + i * HD, HD), HD), :] = half
            send(o.at[k, rows, :], back.at[chip, rows, :], back_send, back_recv)

        @pl.when(k == 7)
        def _():
            @pl.when(p == 0)
            def _():
                wait_bytes(gate_in, gate_recv)

            for i, half in enumerate(halves):
                part = pl.ds(aligned(p * PW + i * HD, HD), HD)
                o_last[part, :] = (gate_in[part, :] * half).astype(BF)
            send(o_last.at[rows, :], gated_v.at[chip, rows, :], last_send, last_recv)

    def rhs_of(chunk, p):
        q = came[p, core, chunk, 2]
        none = jnp.zeros((HD, RES), BF)
        return jnp.concatenate([jnp.concatenate([q[:HD], none], 1), jnp.concatenate([none, q[HD:]], 1)], 0)

    def score_tile(t, rhs, p, chunk, s, top):
        rows = pl.ds(t * TILE, TILE)
        b = jnp.concatenate(
            [
                bias[chunk, half, pl.ds((t * TILE // RES + i) * HALF, HALF), :]
                for i in range(TILE // RES)
                for half in range(2)
            ],
            0,
        ).astype(F32)
        scores = jnp.dot(kn[p, rows, :], rhs, preferred_element_type=F32) + jnp.concatenate([b, b], 1)
        s[rows, :] = scores
        return jnp.maximum(top, jnp.max(scores.reshape(TILE // 8, 8, 2 * RES), axis=0))

    def value_tile(t, p, s, top, total, acc):
        e = jnp.exp(s[pl.ds(t * TILE, TILE), :] - top)
        total = total + jnp.sum(e.reshape(TILE // 8, 8, 2 * RES), axis=0)
        v = [came[p, (t * TILE) // 1024, (t * TILE) % 1024 // RES + i, 1] for i in range(TILE // RES)]
        return total, acc + jnp.dot(jnp.concatenate(v, 1), e.astype(BF), preferred_element_type=F32)

    lowest = jnp.full((8, 2 * RES), -jnp.inf, F32)
    steps = KEYS // TILE
    units = 8 * PAIRS

    def first(s):
        zero = jnp.int32(0)
        before(zero)
        rhs = rhs_of(z, zero)
        top = lowest
        for t in range(steps):
            top = score_tile(t, rhs, zero, z, s, top)
        return top

    def both(u, top, s_now, s_next):
        before(u + 1)
        k, p = place(u)
        kv, pv = place(jnp.minimum(u + 1, units - 1))
        chunk = chunk_of(kv)
        top = jnp.max(top, axis=0, keepdims=True)
        rhs = rhs_of(chunk, pv)
        total = jnp.zeros((8, 2 * RES), F32)
        acc = jnp.zeros((PW, 2 * RES), F32)
        top_next = lowest
        for t in range(steps):
            top_next = score_tile(t, rhs, pv, chunk, s_next, top_next)
            total, acc = value_tile(t, p, s_now, top, total, acc)
        result = acc / jnp.sum(total, axis=0, keepdims=True)
        after(k, p, (result[:HD, :RES], result[HD:, RES:]))
        return top_next

    def body(i, top):
        top = both(2 * i, top, sa, sb)
        return both(2 * i + 1, top, sb, sa)

    lax.fori_loop(0, units // 2, body, first(sa))

    @pl.when(chip != last)
    def _():
        wait_bytes(back, back_recv)
        for h in range(H):
            gated_v[h] = (gate[h] * back[h]).astype(BF)

    @pl.when(chip == last)
    def _():
        wait_bytes(gated_v, last_recv)

    wo = w_v[4]
    for s in range(SEQS):
        gated = jnp.concatenate([gated_v[h, s * HD : (s + 1) * HD, :] for h in range(H)], 0)
        out[s] = jnp.dot(gated.T, wo, preferred_element_type=F32).astype(BF)

    @pl.when(chip != last)
    def _():
        wait_bytes(o.at[pl.ds(0, 6)], back_send)
        wait_bytes(o_last, last_send)

    @pl.when(chip == last)
    def _():
        wait_bytes(o.at[pl.ds(0, 7)], back_send)
        for d in range(1, 8):
            gate_copy(d).wait_send()
    for half in range(2):
        for d in range(8):
            tile_copy(half, d, 1).wait_send()
            if d:
                tile_copy(half, d, 0).wait_send()

        @pl.when(jnp.logical_not(owner))
        def _(half=half):
            tile_copy(half, 0, 0).wait_send()

    for p in range(PAIRS):
        for d in range(1, 8):
            qkv_copy(d, p).wait_send()
        core_copy(p).wait_send()
    for sign in (1, -1):
        for half in range(2):
            for k in range(1, 5):
                if goes(sign, k, half):
                    ring_copy(sign, k, half).wait_send()


def local(x, pair, x_gain, x_shift, pair_gain, wq, wk, wv, wg, gate_shift, w_bias, w_out):
    dma = pltpu.SemaphoreType.DMA
    return pl.pallas_call(
        kernel,
        name="attention",
        out_shape=jax.ShapeDtypeStruct((SEQS, RES, CH), BF),
        in_specs=[HBM, HBM, VMEM, VMEM, VMEM, HBM, HBM, HBM, HBM, VMEM, VMEM, HBM],
        out_specs=VMEM,
        scratch_shapes=[
            pltpu.VMEM((RES, RES, CP), BF),
            pltpu.VMEM((SEQS, RES, CH), BF),
            pltpu.VMEM((5, CH, CH), BF),
            pltpu.VMEM((HALF * H, RES), F32),
            pltpu.VMEM((2, H, HALF, RES), BF),
            pltpu.VMEM((PAIRS, CH, 2 * RES), BF),
            pltpu.VMEM((H, PAIRS, 3, PW, RES), BF),
            pltpu.VMEM((H, ROWS, RES), F32),
            pltpu.VMEM((ROWS, RES), F32),
            pltpu.VMEM((PAIRS, 2, 8, 3, PW, RES), BF),
            pltpu.VMEM((8, 2, KEYS // 2, RES), BF),
            pltpu.VMEM((PAIRS, KEYS, PW), BF),
            pltpu.VMEM((KEYS, 2 * RES), F32),
            pltpu.VMEM((KEYS, 2 * RES), F32),
            pltpu.VMEM((7, ROWS, RES), F32),
            pltpu.VMEM((ROWS, RES), BF),
            pltpu.VMEM((8, ROWS, RES), F32),
            pltpu.VMEM((8, ROWS, RES), BF),
            dma((2, RES // STEP)),
            dma,
            dma((5,)),
            dma((2, 2, 8)),
            dma((PAIRS, 8)),
            dma((8,)),
            dma((PAIRS,)),
            dma((2, 4, 2)),
            dma,
            dma,
            dma((2,)),
            dma((PAIRS,)),
            dma,
            dma((PAIRS,)),
            dma((2, 4, 2)),
            dma,
            dma,
        ],
        compiler_params=pltpu.CompilerParams(
            collective_id=0, has_side_effects=True, vmem_limit_bytes=LIMIT
        ),
    )(
        x, pair, x_gain.reshape(1, CH), x_shift.reshape(1, CH), pair_gain.reshape(1, CP),
        wq, wk, wv, wg, gate_shift.reshape(1, CH), w_bias.T, w_out,
    )


def solution(mesh):
    split = P("seq", "res", None)
    in_specs = (split, split) + (P(),) * 10
    return jax.shard_map(local, mesh=mesh, in_specs=in_specs, out_specs=split, check_vma=False)
```
